256 devices in a mesh: win: 4 (over y_lo, core), tile: 64 (over x, y_hi, z).
Axes of the slice: x: 4, y: 4 (y_hi: 2, y_lo: 2; y = y_hi * 2 + y_lo), z: 8, core: 2. Of those that a mesh axis runs over, the one named last changes fastest.
Arguments:
- state: float32 [4, 64, 5, 32, 8, 128], P('win', 'tile'), may hold values from -6 to 6
- obs_weight: float32 [4, 64, 5, 32, 8, 128], P('win', 'tile'), may hold values from 0 to 1
- trajectory: bfloat16 [4, 64, 3, 2, 32, 8, 128], P('win', 'tile'), may hold values from -0.8984375 to 0.8984375
- coupling: float32 [5, 5], replicated, may hold values from -0.9 to 0.9
- prec_scale: float32 [5, 32], replicated, may hold values from 0.5 to 2
Outputs:
- hess_vec: float32 [4, 64, 5, 32, 8, 128], P('win', 'tile')
The draws below stay inside these ranges and needn't reach their ends.
All inputs are finite; a program needn't handle non-finite values.
Results may differ from the reference program's by a relative error of at most 0.0003.
Values sent between devices are 32-bit elements; how exact they have to be, the bound alone decides.
No kernel may reach another device: no remote copies, remote signals or barrier semaphores. Data moves between devices by JAX's collectives and lax.ppermute only.
A program may use at most 64 MiB of HBM per device.

```python
import math
import jax
import jax.numpy as jnp
from jax import lax

VARS = 5
LEVELS = 32
STEPS = 3
TY = 4
CX = 8
CY = 128
WINDOWS = 4
TILES = 64
XTILES = 16


def shard_levels(stream_key, dims, shards, low, top_value):
    def one(axis_at, blocks):
        heights = jax.random.uniform(jax.random.fold_in(jax.random.fold_in(stream_key, 6), axis_at), (blocks,), jnp.float32, low / len(shards), top_value / len(shards))
        return jnp.repeat(jnp.exp(heights), dims[axis_at] // blocks).reshape((-1,) + (1,) * (len(dims) - axis_at - 1))

    gain = one(*shards[0])
    for cut in shards[1:]:
        gain = gain * one(*cut)
    return gain


def bell_draw(stream_key, extent, scale, most, pieces=(), dtype=jnp.bfloat16):
    array = scale * jax.random.normal(stream_key, extent, jnp.float32)
    if pieces:
        array = array * shard_levels(stream_key, extent, pieces, -0.22, 0.18)
    return jnp.clip(array, -most, most).astype(dtype)


def setup_inputs(seed: int = 0) -> dict:
    streams_of = jax.random.split(jax.random.key(seed), 6)
    return {
        "state": bell_draw(streams_of[0], (WINDOWS, TILES, VARS, LEVELS, CX, CY), 1.0, 6.0, ((0, 4), (1, 64)), jnp.float32),
        "obs_weight": jnp.clip(1.0 * jax.random.uniform(streams_of[1], (WINDOWS, TILES, VARS, LEVELS, CX, CY), jnp.float32) ** shard_levels(streams_of[1], (WINDOWS, TILES, VARS, LEVELS, CX, CY), ((0, 4), (1, 64)), -0.2, 0.2), 0.0, 1.0),
        "trajectory": bell_draw(streams_of[2], (WINDOWS, TILES, STEPS, 2, LEVELS, CX, CY), 0.15, 0.8984375, ((0, 4), (1, 64))),
        "coupling": bell_draw(streams_of[3], (VARS, VARS), 0.15, 0.9, (), jnp.float32),
        "prec_scale": jnp.clip(jnp.exp(jax.random.uniform(streams_of[4], (VARS, LEVELS), jnp.float32, math.log(0.5), math.log(2.0))), 0.5, 2.0),
    }


smooth_weight = 0.2


def to_grid(blocks):
    leading = blocks.shape[1:-2]
    blocks = blocks.reshape((XTILES, TY) + leading + (CX, CY))
    blocks = jnp.moveaxis(blocks, 0, -3)
    blocks = jnp.moveaxis(blocks, 0, -2)
    return blocks.reshape(leading + (XTILES * CX, TY * CY))


def from_grid(field):
    leading = field.shape[:-2]
    field = field.reshape(leading + (XTILES, CX, TY, CY))
    field = jnp.moveaxis(field, -2, 0)
    field = jnp.moveaxis(field, -3, 0)
    return field.reshape((TILES,) + leading + (CX, CY))


def beside(field_x, field_y):
    east_side = jnp.roll(field_x, -1, axis=-2)
    west_side = jnp.roll(field_x, 1, axis=-2)
    north_edge = jnp.roll(field_y[..., :1], -CX, axis=-2)
    south_edge = jnp.roll(field_y[..., -1:], CX, axis=-2)
    north_side = jnp.concatenate([field_y[..., 1:], north_edge], axis=-1)
    south_side = jnp.concatenate([south_edge, field_y[..., :-1]], axis=-1)
    return east_side, west_side, north_side, south_side


def tangent(field, winds, coupling):
    east_side, west_side, north_side, south_side = beside(field, field)
    mixed = jnp.einsum("vw,wlxy->vlxy", coupling, field, precision=lax.Precision.HIGHEST)
    return field + winds[0] * (east_side - west_side) + winds[1] * (north_side - south_side) + mixed


def adjoint(cotangent, winds, coupling):
    east_side, west_side, north_side, south_side = beside(winds[0] * cotangent, winds[1] * cotangent)
    mixed = jnp.einsum("wv,wlxy->vlxy", coupling, cotangent, precision=lax.Precision.HIGHEST)
    return cotangent + (west_side - east_side) + (south_side - north_side) + mixed


def precision_apply(field, prec_scale):
    east_side, west_side, north_side, south_side = beside(field, field)
    stencil = (1.0 + 4.0 * smooth_weight) * field - smooth_weight * (east_side + west_side + north_side + south_side)
    return prec_scale[:, :, None, None] * stencil


def reference(state, obs_weight, trajectory, coupling, prec_scale):
    states = [to_grid(state[window]) for window in range(WINDOWS)]
    moved = []
    for window in range(WINDOWS):
        winds_all = to_grid(trajectory[window])
        field = states[window]
        for step_number in range(STEPS):
            field = tangent(field, winds_all[step_number].astype(jnp.float32), coupling)
        moved.append(field)
    weighted = []
    for window in range(WINDOWS):
        if window == 0:
            mismatch = states[0]
        else:
            mismatch = states[window] - moved[window - 1]
        weighted.append(precision_apply(mismatch, prec_scale))
    outputs = []
    for window in range(WINDOWS):
        result = weighted[window] + to_grid(obs_weight[window]) * states[window]
        if window + 1 < WINDOWS:
            winds_all = to_grid(trajectory[window])
            cotangent = weighted[window + 1]
            for step_number in reversed(range(STEPS)):
                cotangent = adjoint(cotangent, winds_all[step_number].astype(jnp.float32), coupling)
            result = result - cotangent
        outputs.append(from_grid(result))
    return jnp.stack(outputs)
```

```python
import functools

import jax
import jax.numpy as jnp
from jax import lax
from jax.experimental import pallas as pl
from jax.experimental.pallas import tpu as pltpu
from jax.sharding import PartitionSpec as P

VARS = 5
STEPS = 3
GROUP = 16
HALO = 5
TY = 4
OFF = 9
PADDED = OFF + GROUP + OFF
smooth_weight = 0.2


def passed_along(x, axis, by):
    devices = lax.axis_size(axis)
    pairs = [(i, i + by) for i in range(devices) if 0 <= i + by < devices]
    return lax.ppermute(x, axis, pairs)


def shifted(x, axis, by):
    devices = lax.axis_size(axis)
    return lax.ppermute(x, axis, [(i, (i + by) % devices) for i in range(devices)])


def exchange(x):
    groups = [[first + i for i in range(GROUP)] for first in range(0, lax.axis_size("tile"), GROUP)]
    return lax.all_to_all(x, "tile", 0, 0, axis_index_groups=groups, tiled=True)


def masks():
    row = lax.broadcasted_iota(jnp.int32, (8, 128), 0)
    lane = lax.broadcasted_iota(jnp.int32, (8, 128), 1)
    return row == 0, row == 7, lane == 0, lane == 127


def east(sel, here, there):
    return pltpu.roll(jnp.where(sel[0], there, here), 7, 0)


def west(sel, here, there):
    return pltpu.roll(jnp.where(sel[1], there, here), 1, 0)


def north(sel, here, there):
    return pltpu.roll(jnp.where(sel[2], there, here), 127, 1)


def south(sel, here, there):
    return pltpu.roll(jnp.where(sel[3], there, here), 1, 1)


def mixed(coupling, values, a, transposed):
    terms = [(coupling[b, a] if transposed else coupling[a, b]) * values[b] for b in range(VARS)]
    return ((terms[0] + terms[1]) + (terms[2] + terms[3])) + terms[4]


def tangent_step(levels, sel, coupling, src, winds, step, first, last, emit):
    @pl.loop(first, last)
    def _(i):
        for lv in range(levels):
            u = winds[i, (2 * step) * levels + lv]
            v = winds[i, (2 * step + 1) * levels + lv]
            f = [src[i, a * levels + lv] for a in range(VARS)]
            for a in range(VARS):
                k = a * levels + lv
                dx = east(sel, f[a], src[i + TY, k]) - west(sel, f[a], src[i - TY, k])
                dy = north(sel, f[a], src[i + 1, k]) - south(sel, f[a], src[i - 1, k])
                emit(i, k, (f[a] + mixed(coupling, f, a, False)) + (u * dx + v * dy))


def adjoint_step(levels, sel, coupling, src, winds, step, first, last, emit):
    @pl.loop(first, last)
    def _(i):
        for lv in range(levels):
            ku = (2 * step) * levels + lv
            kv = (2 * step + 1) * levels + lv
            ue = east(sel, winds[i, ku], winds[i + TY, ku])
            uw = west(sel, winds[i, ku], winds[i - TY, ku])
            vn = north(sel, winds[i, kv], winds[i + 1, kv])
            vs = south(sel, winds[i, kv], winds[i - 1, kv])
            g = [src[i, a * levels + lv] for a in range(VARS)]
            for a in range(VARS):
                k = a * levels + lv
                flux = uw * west(sel, g[a], src[i - TY, k]) - ue * east(sel, g[a], src[i + TY, k])
                flux += vs * south(sel, g[a], src[i - 1, k]) - vn * north(sel, g[a], src[i + 1, k])
                emit(i, k, (g[a] + mixed(coupling, g, a, True)) + flux)


def precision_step(levels, sel, prec, src, first, last, emit):
    @pl.loop(first, last)
    def _(i):
        for lv in range(levels):
            for a in range(VARS):
                k = a * levels + lv
                f = src[i, k]
                around = east(sel, f, src[i + TY, k]) + west(sel, f, src[i - TY, k])
                around += north(sel, f, src[i + 1, k]) + south(sel, f, src[i - 1, k])
                emit(i, k, prec[a, lv] * ((1.0 + 4.0 * smooth_weight) * f - smooth_weight * around))


def gather_tiles(parts, dst, sems, base):
    west_part, own, east_part = parts
    copies = [
        pltpu.make_async_copy(west_part, dst.at[pl.ds(OFF - HALO, HALO)], sems.at[base]),
        pltpu.make_async_copy(own, dst.at[pl.ds(OFF, GROUP)], sems.at[base + 1]),
        pltpu.make_async_copy(east_part, dst.at[pl.ds(OFF + GROUP, HALO)], sems.at[base + 2]),
    ]
    for copy in copies:
        copy.start()
    return copies


LO, HI = OFF - HALO, OFF + GROUP + HALO


def forward_kernel(levels, window, coupling, prec, sw, so, se, ww, wo, we, fw, fo, fe,
                   full, core, own_weighted, f0, f1, winds, follow, sems):
    sel = masks()
    state_copies = gather_tiles((sw, so, se), f0, sems, 0)
    wind_copies = gather_tiles((ww, wo, we), winds, sems, 3)
    follow_copies = gather_tiles((fw, fo, fe), follow, sems, 6)
    for copy in state_copies + wind_copies + follow_copies:
        copy.wait()

    @pl.when(window[0] == 0)
    def _():
        def emit(i, k, value):
            own_weighted[i - OFF, k] = value

        precision_step(levels, sel, prec, f0, OFF, OFF + GROUP, emit)

    @pl.when(window[0] == window[1])
    def _():
        full[...] = jnp.zeros_like(full)
        core[...] = jnp.zeros_like(core)

    @pl.when(window[0] != window[1])
    def _():
        def into(ref):
            def emit(i, k, value):
                ref[i, k] = value

            return emit

        def mismatch(i, k, value):
            f1[i, k] = follow[i, k] - value

        def weigh(i, k, value):
            full[i - LO, k] = value

        tangent_step(levels, sel, coupling, f0, winds, 0, LO, HI, into(f1))
        tangent_step(levels, sel, coupling, f1, winds, 1, LO, HI, into(f0))
        tangent_step(levels, sel, coupling, f0, winds, 2, LO, HI, mismatch)
        precision_step(levels, sel, prec, f1, LO, HI, weigh)
        core[...] = full[pl.ds(HALO, GROUP)]


def backward_kernel(levels, window, coupling, weighted, ww, wo, we, out, f0, f1, winds, sems):
    sel = masks()
    copies = gather_tiles((ww, wo, we), winds, sems, 0)
    own = pltpu.make_async_copy(weighted, f0.at[pl.ds(LO, HI - LO)], sems.at[3])
    own.start()
    for copy in copies + [own]:
        copy.wait()

    @pl.when(window[0] == window[1])
    def _():
        out[...] = jnp.zeros_like(out)

    @pl.when(window[0] != window[1])
    def _():
        def into(ref):
            def emit(i, k, value):
                ref[i, k] = value

            return emit

        def result(i, k, value):
            out[i - OFF, k] = value

        adjoint_step(levels, sel, coupling, f0, winds, 2, LO, HI, into(f1))
        adjoint_step(levels, sel, coupling, f1, winds, 1, LO + 1, HI - 1, into(f0))
        adjoint_step(levels, sel, coupling, f0, winds, 0, OFF, OFF + GROUP, result)


def with_halo(x):
    return shifted(x[GROUP - HALO :], "tile", GROUP), x, shifted(x[:HALO], "tile", -GROUP)


def body(state, obs_weight, trajectory, coupling, prec_scale):
    own_state = state[0, 0]
    level_count = own_state.shape[1]
    levels = level_count // GROUP
    cell = own_state.shape[2:]
    window_index = lax.axis_index("win")
    last_window = lax.axis_size("win") - 1
    window = jnp.stack([window_index, jnp.int32(last_window)]).astype(jnp.int32)
    first_level = (lax.axis_index("tile") % GROUP) * levels
    prec = lax.dynamic_slice_in_dim(prec_scale, first_level, levels, axis=1)

    def by_level(x):
        kinds = x.shape[0]
        x = x.reshape((kinds, GROUP, levels) + cell)
        return jnp.moveaxis(x, 1, 0).reshape((GROUP, kinds * levels) + cell)

    slab = exchange(by_level(own_state))
    slab_parts = with_halo(slab)
    follow_core = passed_along(slab, "win", -1)
    winds = exchange(by_level(trajectory[0, 0].reshape((2 * STEPS, level_count) + cell).astype(jnp.float32)))
    wind_parts = with_halo(winds)
    follow_parts = (passed_along(slab_parts[0], "win", -1), follow_core, passed_along(slab_parts[2], "win", -1))

    fields = VARS * levels
    smem = pl.BlockSpec(memory_space=pltpu.SMEM)
    anyspace = pl.BlockSpec(memory_space=pl.ANY)
    vmem = pl.BlockSpec(memory_space=pltpu.VMEM)
    padded = pltpu.VMEM((PADDED, fields) + cell, jnp.float32)
    padded_winds = pltpu.VMEM((PADDED, 2 * STEPS * levels) + cell, jnp.float32)
    core_shape = jax.ShapeDtypeStruct((GROUP, fields) + cell, jnp.float32)
    full_shape = jax.ShapeDtypeStruct((HI - LO, fields) + cell, jnp.float32)
    full, core, own_weighted = pl.pallas_call(
        functools.partial(forward_kernel, levels),
        out_shape=(full_shape, core_shape, core_shape),
        in_specs=[smem] * 3 + [anyspace] * 9,
        out_specs=(vmem,) * 3,
        scratch_shapes=[padded, padded, padded_winds, padded, pltpu.SemaphoreType.DMA((9,))],
        compiler_params=pltpu.CompilerParams(vmem_limit_bytes=40 * 2**20),
        name="forward",
    )(window, coupling, prec, *slab_parts, *wind_parts, *follow_parts)
    earlier = passed_along(core, "win", 1)
    cotangent = pl.pallas_call(
        functools.partial(backward_kernel, levels),
        out_shape=core_shape,
        in_specs=[smem] * 2 + [anyspace] * 4,
        out_specs=vmem,
        scratch_shapes=[padded, padded, padded_winds, pltpu.SemaphoreType.DMA((4,))],
        compiler_params=pltpu.CompilerParams(vmem_limit_bytes=40 * 2**20),
        cost_estimate=pl.CostEstimate(flops=20_000_000, bytes_accessed=4_000_000, transcendentals=0),
        name="backward",
    )(window, coupling, full, *wind_parts)
    weighted = jnp.where(window_index == 0, own_weighted, earlier)
    back = exchange(weighted - cotangent)
    back = jnp.moveaxis(back.reshape((GROUP, VARS, levels) + cell), 0, 1).reshape(own_state.shape)
    return (back + obs_weight[0, 0] * own_state)[None, None]


def solution(mesh):
    in_specs = (
        P("win", "tile", None, None, None, None),
        P("win", "tile", None, None, None, None),
        P("win", "tile", None, None, None, None, None),
        P(),
        P(),
    )
    out_specs = P("win", "tile", None, None, None, None)
    return jax.shard_map(body, mesh=mesh, in_specs=in_specs, out_specs=out_specs, check_vma=False)
```

```python
import functools

import jax
import jax.numpy as jnp
from jax import lax
from jax.experimental import pallas as pl
from jax.experimental.pallas import tpu as pltpu
from jax.sharding import PartitionSpec as P

VARS = 5
STEPS = 3
GROUP = 16
HALO = 5
TY = 4
OFF = 9
PADDED = OFF + GROUP + OFF
UNROLL = {26: 13, 24: 8, 16: 8}
SPLIT = 1
smooth_weight = 0.2


def passed_along(x, axis, by):
    devices = lax.axis_size(axis)
    pairs = [(i, i + by) for i in range(devices) if 0 <= i + by < devices]
    return lax.ppermute(x, axis, pairs)


def shifted(x, axis, by):
    devices = lax.axis_size(axis)
    return lax.ppermute(x, axis, [(i, (i + by) % devices) for i in range(devices)])


def exchange(x):
    groups = [[first + i for i in range(GROUP)] for first in range(0, lax.axis_size("tile"), GROUP)]
    return lax.all_to_all(x, "tile", 0, 0, axis_index_groups=groups, tiled=True)


def masks():
    row = lax.broadcasted_iota(jnp.int32, (8, 128), 0)
    lane = lax.broadcasted_iota(jnp.int32, (8, 128), 1)
    return row == 0, row == 7, lane == 0, lane == 127


def east(sel, here, there):
    return pltpu.roll(jnp.where(sel[0], there, here), 7, 0)


def west(sel, here, there):
    return pltpu.roll(jnp.where(sel[1], there, here), 1, 0)


def north(sel, here, there):
    return pltpu.roll(jnp.where(sel[2], there, here), 127, 1)


def south(sel, here, there):
    return pltpu.roll(jnp.where(sel[3], there, here), 1, 1)


def mixed(coupling, values, a, transposed):
    terms = [(coupling[b, a] if transposed else coupling[a, b]) * values[b] for b in range(VARS)]
    return ((terms[0] + terms[1]) + (terms[2] + terms[3])) + terms[4]


def tangent_step(levels, sel, coupling, src, winds, step, first, last, emit):
    @pl.loop(first, last, unroll=UNROLL[last - first])
    def _(i):
        for lv in range(levels):
            u = winds[i, (2 * step) * levels + lv]
            v = winds[i, (2 * step + 1) * levels + lv]
            f = [src[i, a * levels + lv] for a in range(VARS)]
            for a in range(VARS):
                k = a * levels + lv
                dx = east(sel, f[a], src[i + TY, k]) - west(sel, f[a], src[i - TY, k])
                dy = north(sel, f[a], src[i + 1, k]) - south(sel, f[a], src[i - 1, k])
                emit(i, k, (f[a] + mixed(coupling, f, a, False)) + (u * dx + v * dy))


def adjoint_step(levels, sel, coupling, src, winds, step, first, last, emit):
    @pl.loop(first, last, unroll=UNROLL[last - first])
    def _(i):
        for lv in range(levels):
            ku = (2 * step) * levels + lv
            kv = (2 * step + 1) * levels + lv
            ue = east(sel, winds[i, ku], winds[i + TY, ku])
            uw = west(sel, winds[i, ku], winds[i - TY, ku])
            vn = north(sel, winds[i, kv], winds[i + 1, kv])
            vs = south(sel, winds[i, kv], winds[i - 1, kv])
            g = [src[i, a * levels + lv] for a in range(VARS)]
            for a in range(VARS):
                k = a * levels + lv
                flux = uw * west(sel, g[a], src[i - TY, k]) - ue * east(sel, g[a], src[i + TY, k])
                flux += vs * south(sel, g[a], src[i - 1, k]) - vn * north(sel, g[a], src[i + 1, k])
                emit(i, k, (g[a] + mixed(coupling, g, a, True)) + flux)


def precision_step(levels, sel, prec, src, first, last, emit):
    @pl.loop(first, last, unroll=UNROLL[last - first])
    def _(i):
        for lv in range(levels):
            for a in range(VARS):
                k = a * levels + lv
                f = src[i, k]
                around = east(sel, f, src[i + TY, k]) + west(sel, f, src[i - TY, k])
                around += north(sel, f, src[i + 1, k]) + south(sel, f, src[i - 1, k])
                emit(i, k, prec[a, lv] * ((1.0 + 4.0 * smooth_weight) * f - smooth_weight * around))


def gather_tiles(parts, first, dst, sems, base):
    planes = pl.ds(first, dst.shape[1])
    west_part, own, east_part = [part.at[:, planes] for part in parts]
    copies = [
        pltpu.make_async_copy(west_part, dst.at[pl.ds(OFF - HALO, HALO)], sems.at[base]),
        pltpu.make_async_copy(own, dst.at[pl.ds(OFF, GROUP)], sems.at[base + 1]),
        pltpu.make_async_copy(east_part, dst.at[pl.ds(OFF + GROUP, HALO)], sems.at[base + 2]),
    ]
    for copy in copies:
        copy.start()
    return copies


LO, HI = OFF - HALO, OFF + GROUP + HALO


def forward_kernel(levels, window, coupling, prec, west_in, own_in, east_in, fw, fo, fe,
                   full, core, own_weighted, f0, f1, winds, follow, sems):
    sel = masks()
    parts = (west_in, own_in, east_in)
    state_copies = gather_tiles(parts, 0, f0, sems, 0)
    wind_copies = gather_tiles(parts, VARS * levels, winds, sems, 3)
    follow_copies = gather_tiles((fw, fo, fe), 0, follow, sems, 6)
    for copy in state_copies + wind_copies + follow_copies:
        copy.wait()

    @pl.when(window[0] == 0)
    def _():
        def emit(i, k, value):
            own_weighted[i - OFF, k] = value

        precision_step(levels, sel, prec, f0, OFF, OFF + GROUP, emit)

    @pl.when(window[0] == window[1])
    def _():
        full[...] = jnp.zeros_like(full)
        core[...] = jnp.zeros_like(core)

    @pl.when(window[0] != window[1])
    def _():
        def into(ref):
            def emit(i, k, value):
                ref[i, k] = value

            return emit

        def mismatch(i, k, value):
            f1[i, k] = follow[i, k] - value

        def weigh(i, k, value):
            full[i - LO, k] = value

        tangent_step(levels, sel, coupling, f0, winds, 0, LO, HI, into(f1))
        tangent_step(levels, sel, coupling, f1, winds, 1, LO, HI, into(f0))
        tangent_step(levels, sel, coupling, f0, winds, 2, LO, HI, mismatch)
        precision_step(levels, sel, prec, f1, LO, HI, weigh)
        core[...] = full[pl.ds(HALO, GROUP)]


def backward_kernel(levels, window, coupling, weighted, west_in, own_in, east_in, out, f0, f1, winds, sems):
    sel = masks()
    copies = gather_tiles((west_in, own_in, east_in), VARS * levels, winds, sems, 0)
    own = pltpu.make_async_copy(weighted, f0.at[pl.ds(LO, HI - LO)], sems.at[3])
    own.start()
    for copy in copies + [own]:
        copy.wait()

    @pl.when(window[0] == window[1])
    def _():
        out[...] = jnp.zeros_like(out)

    @pl.when(window[0] != window[1])
    def _():
        def into(ref):
            def emit(i, k, value):
                ref[i, k] = value

            return emit

        def result(i, k, value):
            out[i - OFF, k] = value

        adjoint_step(levels, sel, coupling, f0, winds, 2, LO, HI, into(f1))
        adjoint_step(levels, sel, coupling, f1, winds, 1, LO + 1, HI - 1, into(f0))
        adjoint_step(levels, sel, coupling, f0, winds, 0, OFF, OFF + GROUP, result)


def with_halo(x):
    return shifted(x[GROUP - HALO :], "tile", GROUP), x, shifted(x[:HALO], "tile", -GROUP)


def chunk_apply(own_state, winds, coupling, prec_scale, half):
    levels = own_state.shape[1] // GROUP
    cell = own_state.shape[2:]
    fields = VARS * levels
    window_index = lax.axis_index("win")
    last_window = lax.axis_size("win") - 1
    window = jnp.stack([window_index, jnp.int32(last_window)]).astype(jnp.int32)
    first_level = (half * GROUP + lax.axis_index("tile") % GROUP) * levels
    prec = lax.dynamic_slice_in_dim(prec_scale, first_level, levels, axis=1)

    def by_level(x):
        kinds = x.shape[0]
        x = x.reshape((kinds, GROUP, levels) + cell)
        return jnp.moveaxis(x, 1, 0).reshape((GROUP, kinds * levels) + cell)

    slab = exchange(by_level(jnp.concatenate([own_state, winds])))
    parts = with_halo(slab)
    follow_parts = [passed_along(part[:, :fields], "win", -1) for part in parts]

    smem = pl.BlockSpec(memory_space=pltpu.SMEM)
    anyspace = pl.BlockSpec(memory_space=pl.ANY)
    vmem = pl.BlockSpec(memory_space=pltpu.VMEM)
    padded = pltpu.VMEM((PADDED, fields) + cell, jnp.float32)
    padded_winds = pltpu.VMEM((PADDED, 2 * STEPS * levels) + cell, jnp.float32)
    core_shape = jax.ShapeDtypeStruct((GROUP, fields) + cell, jnp.float32)
    full_shape = jax.ShapeDtypeStruct((HI - LO, fields) + cell, jnp.float32)
    full, core, own_weighted = pl.pallas_call(
        functools.partial(forward_kernel, levels),
        out_shape=(full_shape, core_shape, core_shape),
        in_specs=[smem] * 3 + [anyspace] * 6,
        out_specs=(vmem,) * 3,
        scratch_shapes=[padded, padded, padded_winds, padded, pltpu.SemaphoreType.DMA((9,))],
        compiler_params=pltpu.CompilerParams(vmem_limit_bytes=24 * 2**20),
        cost_estimate=pl.CostEstimate(flops=8_000_000 * levels, bytes_accessed=8_000_000 * levels, transcendentals=0),
        name="forward",
    )(window, coupling, prec, *parts, *follow_parts)
    earlier = passed_along(core, "win", 1)
    cotangent = pl.pallas_call(
        functools.partial(backward_kernel, levels),
        out_shape=core_shape,
        in_specs=[smem] * 2 + [anyspace] * 4,
        out_specs=vmem,
        scratch_shapes=[padded, padded, padded_winds, pltpu.SemaphoreType.DMA((4,))],
        compiler_params=pltpu.CompilerParams(vmem_limit_bytes=24 * 2**20),
        cost_estimate=pl.CostEstimate(flops=6_000_000 * levels, bytes_accessed=6_000_000 * levels, transcendentals=0),
        name="backward",
    )(window, coupling, full, *parts)
    weighted = jnp.where(window_index == 0, own_weighted, earlier)
    back = exchange(weighted - cotangent)
    return jnp.moveaxis(back.reshape((GROUP, VARS, levels) + cell), 0, 1).reshape(own_state.shape)


def body(state, obs_weight, trajectory, coupling, prec_scale):
    own_state = state[0, 0]
    level_count = own_state.shape[1]
    winds = trajectory[0, 0].reshape((2 * STEPS,) + own_state.shape[1:]).astype(jnp.float32)
    part = level_count // SPLIT
    pieces = []
    for half in range(SPLIT):
        at = slice(half * part, (half + 1) * part)
        pieces.append(chunk_apply(own_state[:, at], winds[:, at], coupling, prec_scale, half))
    back = jnp.concatenate(pieces, axis=1)
    return (back + obs_weight[0, 0] * own_state)[None, None]


def solution(mesh):
    in_specs = (
        P("win", "tile", None, None, None, None),
        P("win", "tile", None, None, None, None),
        P("win", "tile", None, None, None, None, None),
        P(),
        P(),
    )
    out_specs = P("win", "tile", None, None, None, None)
    return jax.shard_map(body, mesh=mesh, in_specs=in_specs, out_specs=out_specs, check_vma=False)
```

```python
import functools

import jax
import jax.numpy as jnp
from jax import lax
from jax.experimental import pallas as pl
from jax.experimental.pallas import tpu as pltpu
from jax.sharding import PartitionSpec as P

VARS = 5
STEPS = 3
GROUP = 16
HALO = 5
TY = 4
smooth_weight = 0.2


def passed_along(x, axis, by):
    devices = lax.axis_size(axis)
    pairs = [(i, i + by) for i in range(devices) if 0 <= i + by < devices]
    return lax.ppermute(x, axis, pairs)


def shifted(x, axis, by):
    devices = lax.axis_size(axis)
    return lax.ppermute(x, axis, [(i, (i + by) % devices) for i in range(devices)])


def exchange(x):
    groups = [[first + i for i in range(GROUP)] for first in range(0, lax.axis_size("tile"), GROUP)]
    return lax.all_to_all(x, "tile", 0, 0, axis_index_groups=groups, tiled=True)


def masks():
    row = lax.broadcasted_iota(jnp.int32, (8, 128), 0)
    lane = lax.broadcasted_iota(jnp.int32, (8, 128), 1)
    return row == 0, row == 7, lane == 0, lane == 127


def east(sel, here, there):
    return pltpu.roll(jnp.where(sel[0], there, here), 7, 0)


def west(sel, here, there):
    return pltpu.roll(jnp.where(sel[1], there, here), 1, 0)


def north(sel, here, there):
    return pltpu.roll(jnp.where(sel[2], there, here), 127, 1)


def south(sel, here, there):
    return pltpu.roll(jnp.where(sel[3], there, here), 1, 1)


def mixed(coupling, values, a, transposed):
    terms = [(coupling[b, a] if transposed else coupling[a, b]) * values[b] for b in range(VARS)]
    return ((terms[0] + terms[1]) + (terms[2] + terms[3])) + terms[4]


class Slab:
    def __init__(self, parts, first=0):
        self.parts, self.first = parts, first

    def __getitem__(self, at):
        j, k = at
        ref, n = self.place(j)
        return ref[n, self.first + k]

    def place(self, j):
        west_part, own, east_part = self.parts
        if j < 0:
            return west_part, max(j + HALO, 0)
        if j < GROUP:
            return own, j
        return east_part, min(j - GROUP, HALO - 1)

    def put(self, j, k, value):
        ref, n = self.place(j)
        ref[n, k] = value


def tangent_step(levels, sel, coupling, src, winds, step, tiles, emit):
    @pl.loop(0, levels)
    def _(lv):
        for j in tiles:
            u = winds[j, 2 * step * levels + lv]
            v = winds[j, (2 * step + 1) * levels + lv]
            f = [src[j, a * levels + lv] for a in range(VARS)]
            for a in range(VARS):
                k = a * levels + lv
                dx = east(sel, f[a], src[j + TY, k]) - west(sel, f[a], src[j - TY, k])
                dy = north(sel, f[a], src[j + 1, k]) - south(sel, f[a], src[j - 1, k])
                emit(j, k, (f[a] + mixed(coupling, f, a, False)) + (u * dx + v * dy))


def adjoint_step(levels, sel, coupling, src, winds, step, tiles, emit):
    @pl.loop(0, levels)
    def _(lv):
        ku = 2 * step * levels + lv
        kv = (2 * step + 1) * levels + lv
        for j in tiles:
            ue = east(sel, winds[j, ku], winds[j + TY, ku])
            uw = west(sel, winds[j, ku], winds[j - TY, ku])
            vn = north(sel, winds[j, kv], winds[j + 1, kv])
            vs = south(sel, winds[j, kv], winds[j - 1, kv])
            g = [src[j, a * levels + lv] for a in range(VARS)]
            for a in range(VARS):
                k = a * levels + lv
                flux = uw * west(sel, g[a], src[j - TY, k]) - ue * east(sel, g[a], src[j + TY, k])
                flux += vs * south(sel, g[a], src[j - 1, k]) - vn * north(sel, g[a], src[j + 1, k])
                emit(j, k, (g[a] + mixed(coupling, g, a, True)) + flux)


def precision_step(levels, sel, prec, src, tiles, emit):
    @pl.loop(0, levels)
    def _(lv):
        for j in tiles:
            for a in range(VARS):
                k = a * levels + lv
                f = src[j, k]
                around = east(sel, f, src[j + TY, k]) + west(sel, f, src[j - TY, k])
                around += north(sel, f, src[j + 1, k]) + south(sel, f, src[j - 1, k])
                emit(j, k, prec[a, lv] * ((1.0 + 4.0 * smooth_weight) * f - smooth_weight * around))


OWN = range(GROUP)
WEST, EAST = range(-HALO, 0), range(GROUP, GROUP + HALO)
ALL = range(-HALO, GROUP + HALO)


def put_in(ref):
    def emit(j, k, value):
        ref[j, k] = value

    return emit


def forward_kernel(levels, window, coupling, prec, west_in, own_in, east_in, *refs):
    sel = masks()
    parts = (west_in, own_in, east_in)
    state, winds = Slab(parts), Slab(parts, VARS * levels)
    moved, weighed, f0, f1 = Slab(refs[:3]), refs[3], Slab(refs[4:7]), Slab(refs[7:10])

    @pl.when(window[0] != window[1])
    def _():
        tangent_step(levels, sel, coupling, state, winds, 0, ALL, f0.put)
        tangent_step(levels, sel, coupling, f0, winds, 1, ALL, f1.put)
        tangent_step(levels, sel, coupling, f1, winds, 2, ALL, moved.put)
        precision_step(levels, sel, prec, moved, OWN, put_in(weighed))


def backward_kernel(levels, window, coupling, prec, follow_own, follow_halo, *refs):
    sel = masks()
    moved, parts, out = Slab(refs[:3]), refs[3:6], refs[6]
    f0, f1 = Slab(refs[7:10]), Slab(refs[10:13])
    state, winds = Slab(parts), Slab(parts, VARS * levels)
    follow = Slab((follow_halo.at[pl.ds(0, HALO)], follow_own, follow_halo.at[pl.ds(HALO, HALO)]))

    precision_step(levels, sel, prec, state, OWN, put_in(out))

    @pl.when(window[0] != window[1])
    def _():
        def result(j, k, value):
            out[j, k] = out[j, k] - value

        @pl.loop(0, VARS * levels)
        def _(k):
            for j in ALL:
                f1.put(j, k, follow[j, k] - moved[j, k])

        precision_step(levels, sel, prec, f1, ALL, f0.put)
        adjoint_step(levels, sel, coupling, f0, winds, 2, ALL, f1.put)
        adjoint_step(levels, sel, coupling, f1, winds, 1, ALL[1:-1], f0.put)
        adjoint_step(levels, sel, coupling, f0, winds, 0, OWN, result)


def with_halo(x):
    return shifted(x[GROUP - HALO :], "tile", GROUP), x, shifted(x[:HALO], "tile", -GROUP)


def body(state, obs_weight, trajectory, coupling, prec_scale):
    own_state = state[0, 0]
    levels = own_state.shape[1] // GROUP
    cell = own_state.shape[2:]
    winds = trajectory[0, 0].reshape((2 * STEPS,) + own_state.shape[1:]).astype(jnp.float32)
    fields = VARS * levels
    window_index = lax.axis_index("win")
    last_window = lax.axis_size("win") - 1
    window = jnp.stack([window_index, jnp.int32(last_window)]).astype(jnp.int32)
    prec = lax.dynamic_slice_in_dim(prec_scale, (lax.axis_index("tile") % GROUP) * levels, levels, axis=1)

    def by_level(x):
        kinds = x.shape[0]
        x = x.reshape((kinds, GROUP, levels) + cell)
        return jnp.moveaxis(x, 1, 0).reshape((GROUP, kinds * levels) + cell)

    slab = exchange(by_level(jnp.concatenate([own_state, winds])))
    parts = with_halo(slab)
    follow_own = passed_along(slab[:, :fields], "win", -1)
    follow_halo = passed_along(jnp.concatenate([parts[0][:, :fields], parts[2][:, :fields]]), "win", -1)

    smem = pl.BlockSpec(memory_space=pltpu.SMEM)
    vmem = pl.BlockSpec(memory_space=pltpu.VMEM)
    core_shape = jax.ShapeDtypeStruct((GROUP, fields) + cell, jnp.float32)
    halo_shape = jax.ShapeDtypeStruct((HALO, fields) + cell, jnp.float32)
    slab_shapes = (halo_shape, core_shape, halo_shape)
    slab_scratch = [pltpu.VMEM(x.shape, x.dtype) for x in slab_shapes]
    params = pltpu.CompilerParams(vmem_limit_bytes=12 * 2**20)

    def cost(flops, moved_bytes):
        return pl.CostEstimate(flops=flops, bytes_accessed=moved_bytes, transcendentals=0)

    *moved, weighed = pl.pallas_call(
        functools.partial(forward_kernel, levels),
        out_shape=slab_shapes + (core_shape,),
        in_specs=[smem] * 3 + [vmem] * 3,
        out_specs=(vmem,) * 4,
        scratch_shapes=slab_scratch * 2,
        compiler_params=params,
        cost_estimate=cost(10_000_000, 12_000_000),
        name="forward",
    )(window, coupling, prec, *parts)
    earlier = passed_along(weighed, "win", 1)
    partial = pl.pallas_call(
        functools.partial(backward_kernel, levels),
        out_shape=core_shape,
        in_specs=[smem] * 3 + [vmem] * 8,
        out_specs=vmem,
        scratch_shapes=slab_scratch * 2,
        compiler_params=params,
        cost_estimate=cost(12_000_000, 14_000_000),
        name="backward",
    )(window, coupling, prec, follow_own, follow_halo, *moved, *parts)
    back = exchange(partial - earlier)
    back = jnp.moveaxis(back.reshape((GROUP, VARS, levels) + cell), 0, 1).reshape(own_state.shape)
    return (back + obs_weight[0, 0] * own_state)[None, None]


def solution(mesh):
    in_specs = (
        P("win", "tile", None, None, None, None),
        P("win", "tile", None, None, None, None),
        P("win", "tile", None, None, None, None, None),
        P(),
        P(),
    )
    out_specs = P("win", "tile", None, None, None, None)
    return jax.shard_map(body, mesh=mesh, in_specs=in_specs, out_specs=out_specs, check_vma=False)
```

```python
import functools

import jax
import jax.numpy as jnp
from jax import lax
from jax.experimental import pallas as pl
from jax.experimental.pallas import tpu as pltpu
from jax.sharding import PartitionSpec as P

VARS = 5
STEPS = 3
GROUP = 16
TY = 4
HALO = TY + 1
CORNER = 8
smooth_weight = 0.2


def passed_along(x, axis, by):
    devices = lax.axis_size(axis)
    pairs = [(i, i + by) for i in range(devices) if 0 <= i + by < devices]
    return lax.ppermute(x, axis, pairs)


def shifted(x, axis, by):
    devices = lax.axis_size(axis)
    return lax.ppermute(x, axis, [(i, (i + by) % devices) for i in range(devices)])


def exchange(x):
    groups = [[first + i for i in range(GROUP)] for first in range(0, lax.axis_size("tile"), GROUP)]
    return lax.all_to_all(x, "tile", 0, 0, axis_index_groups=groups, tiled=True)


def masks():
    row = lax.broadcasted_iota(jnp.int32, (8, 128), 0)
    lane = lax.broadcasted_iota(jnp.int32, (8, 128), 1)
    return row == 0, row == 7, lane == 0, lane == 127


def east(sel, here, there):
    return pltpu.roll(jnp.where(sel[0], there, here), 7, 0)


def west(sel, here, there):
    return pltpu.roll(jnp.where(sel[1], there, here), 1, 0)


def north(sel, here, there):
    return pltpu.roll(jnp.where(sel[2], there, here), 127, 1)


def south(sel, here, there):
    return pltpu.roll(jnp.where(sel[3], there, here), 1, 1)


def mixed(coupling, values, a, transposed):
    terms = [(coupling[b, a] if transposed else coupling[a, b]) * values[b] for b in range(VARS)]
    return ((terms[0] + terms[1]) + (terms[2] + terms[3])) + terms[4]


class Slab:
    def __init__(self, parts, first=0):
        self.parts, self.first = parts, first

    def __getitem__(self, at):
        j, k = at
        ref, n = self.place(j)
        return ref[n, self.first + k]

    def place(self, j):
        west_part, own, east_part = self.parts
        if j < 0:
            return west_part, max(j + HALO, 0)
        if j < GROUP:
            return own, j
        return east_part, min(j - GROUP, HALO - 1)

    def put(self, j, k, value):
        ref, n = self.place(j)
        ref[n, k] = value


class Received:
    def __init__(self, west_packed, west_corner, own, east_packed, east_corner, first=0):
        self.west, self.east = (west_packed, west_corner), (east_packed, east_corner)
        self.own, self.first, self.planes = own, first, own.shape[1]

    def __getitem__(self, at):
        j, k = at[0], self.first + at[1]
        if j < -TY:
            return self.west[1][k]
        if j < 0:
            return self.west[0][(j + TY) * self.planes + k]
        if j < GROUP:
            return self.own[j, k]
        if j < GROUP + TY:
            return self.east[0][(j - GROUP) * self.planes + k]
        return self.east[1][k]


def tangent_step(levels, sel, coupling, src, winds, step, tiles, emit):
    @pl.loop(0, levels)
    def _(lv):
        for j in tiles:
            u = winds[j, 2 * step * levels + lv]
            v = winds[j, (2 * step + 1) * levels + lv]
            f = [src[j, a * levels + lv] for a in range(VARS)]
            for a in range(VARS):
                k = a * levels + lv
                dx = east(sel, f[a], src[j + TY, k]) - west(sel, f[a], src[j - TY, k])
                dy = north(sel, f[a], src[j + 1, k]) - south(sel, f[a], src[j - 1, k])
                emit(j, k, (f[a] + mixed(coupling, f, a, False)) + (u * dx + v * dy))


def adjoint_step(levels, sel, coupling, src, winds, step, tiles, emit):
    @pl.loop(0, levels)
    def _(lv):
        ku = 2 * step * levels + lv
        kv = (2 * step + 1) * levels + lv
        for j in tiles:
            ue = east(sel, winds[j, ku], winds[j + TY, ku])
            uw = west(sel, winds[j, ku], winds[j - TY, ku])
            vn = north(sel, winds[j, kv], winds[j + 1, kv])
            vs = south(sel, winds[j, kv], winds[j - 1, kv])
            g = [src[j, a * levels + lv] for a in range(VARS)]
            for a in range(VARS):
                k = a * levels + lv
                flux = uw * west(sel, g[a], src[j - TY, k]) - ue * east(sel, g[a], src[j + TY, k])
                flux += vs * south(sel, g[a], src[j - 1, k]) - vn * north(sel, g[a], src[j + 1, k])
                emit(j, k, (g[a] + mixed(coupling, g, a, True)) + flux)


def precision_step(levels, sel, prec, src, tiles, emit):
    @pl.loop(0, levels)
    def _(lv):
        for j in tiles:
            for a in range(VARS):
                k = a * levels + lv
                f = src[j, k]
                around = east(sel, f, src[j + TY, k]) + west(sel, f, src[j - TY, k])
                around += north(sel, f, src[j + 1, k]) + south(sel, f, src[j - 1, k])
                emit(j, k, prec[a, lv] * ((1.0 + 4.0 * smooth_weight) * f - smooth_weight * around))


OWN = range(GROUP)
WEST, EAST = range(-HALO, 0), range(GROUP, GROUP + HALO)
ALL = range(-HALO, GROUP + HALO)


def put_in(ref):
    def emit(j, k, value):
        ref[j, k] = value

    return emit


SLOTS = 128 // CORNER


def pack_corner(tile, out, at, shift):
    slot = lax.broadcasted_iota(jnp.int32, (8, 128), 1) // CORNER
    for first in range(0, len(tile), SLOTS):
        packed = jnp.zeros((8, 128), jnp.float32)
        for q, plane in enumerate(tile[first : first + SLOTS]):
            packed = jnp.where(slot == q, pltpu.roll(plane, (CORNER * q + shift) % 128, 1), packed)
        out[at + first // SLOTS] = packed


def unpack_corner(packed, at, out, shift):
    for k in range(out.shape[0]):
        out[k] = pltpu.roll(packed[at + k // SLOTS], (-CORNER * (k % SLOTS) - shift) % 128, 1)


def pack_kernel(fields, own, east_going, west_going, follow_east_going, follow_west_going):
    top = lax.broadcasted_iota(jnp.int32, (8, 128), 0) < 4
    count = own.shape[1]
    half = fields // 2
    for out, follow_out, first, paired, whole, corner, shift in (
        (east_going, follow_east_going, GROUP - TY, GROUP - TY, GROUP - 1, GROUP - HALO, CORNER),
        (west_going, follow_west_going, 0, 1, 0, TY, 0),
    ):
        for n in range(TY):
            out[pl.ds(n * count, count)] = own[first + n]
        follow_out[pl.ds((TY - 1) * half, fields)] = own[whole, pl.ds(0, fields)]
        for n in range(TY - 1):
            for k in range(0, fields, 2):
                one, two = own[paired + n, k], own[paired + n, k + 1]
                if shift:
                    pair = jnp.where(top, pltpu.roll(one, 4, 0), two)
                else:
                    pair = jnp.where(top, one, pltpu.roll(two, 4, 0))
                follow_out[n * half + k // 2] = pair
        tile = [own[corner, k] for k in range(count)]
        pack_corner(tile, out, TY * count, shift)
        pack_corner(tile[:fields], follow_out, (TY + 1) * half, shift)


def put_in(ref):
    def emit(j, k, value):
        ref[j, k] = value

    return emit


def received(west_in, own_in, east_in, west_corner, east_corner, first):
    at = TY * own_in.shape[1]
    unpack_corner(west_in, at, west_corner, CORNER)
    unpack_corner(east_in, at, east_corner, 0)
    return [Received(west_in, west_corner, own_in, east_in, east_corner, f) for f in (0, first)]


def forward_kernel(levels, window, coupling, prec, west_in, own_in, east_in, *refs):
    refs = refs[2:]
    sel = masks()
    moved, weighed, f0, f1 = Slab(refs[:3]), refs[3], Slab(refs[4:7]), Slab(refs[7:10])
    state, winds = received(west_in, own_in, east_in, *refs[10:12], VARS * levels)

    @pl.when(window[0] != window[1])
    def _():
        tangent_step(levels, sel, coupling, state, winds, 0, ALL, f0.put)
        tangent_step(levels, sel, coupling, f0, winds, 1, ALL, f1.put)
        tangent_step(levels, sel, coupling, f1, winds, 2, ALL, moved.put)
        precision_step(levels, sel, prec, moved, OWN, put_in(weighed))


def backward_kernel(levels, window, coupling, prec, follow_west, follow_own, follow_east, *refs):
    sel = masks()
    moved, out = Slab(refs[:3]), refs[6]
    f0, f1 = Slab(refs[7:10]), Slab(refs[10:13])
    state, winds = received(*refs[3:6], *refs[13:15], VARS * levels)
    fields = VARS * levels

    precision_step(levels, sel, prec, state, OWN, put_in(out))

    @pl.when(window[0] != window[1])
    def _():
        def result(j, k, value):
            out[j, k] = out[j, k] - value

        half = fields // 2
        for k in range(fields):
            for n in range(TY - 1):
                west_pair, east_pair = follow_west[n * half + k // 2], follow_east[n * half + k // 2]
                if k % 2 == 0:
                    west_pair = pltpu.roll(west_pair, 4, 0)
                else:
                    east_pair = pltpu.roll(east_pair, 4, 0)
                f1.put(n - TY, k, west_pair - moved[n - TY, k])
                f1.put(GROUP + 1 + n, k, east_pair - moved[GROUP + 1 + n, k])
            f1.put(-1, k, follow_west[(TY - 1) * half + k] - moved[-1, k])
            f1.put(GROUP, k, follow_east[(TY - 1) * half + k] - moved[GROUP, k])
            at, turn = (TY + 1) * half + k // SLOTS, CORNER * (k % SLOTS)
            f1.put(-HALO, k, pltpu.roll(follow_west[at], (-turn - CORNER) % 128, 1) - moved[-HALO, k])
            f1.put(GROUP + TY, k, pltpu.roll(follow_east[at], -turn % 128, 1) - moved[GROUP + TY, k])

        @pl.loop(0, fields)
        def _(k):
            for j in OWN:
                f1.put(j, k, follow_own[j, k] - moved[j, k])

        precision_step(levels, sel, prec, f1, ALL, f0.put)
        adjoint_step(levels, sel, coupling, f0, winds, 2, ALL, f1.put)
        adjoint_step(levels, sel, coupling, f1, winds, 1, ALL[1:-1], f0.put)
        adjoint_step(levels, sel, coupling, f0, winds, 0, OWN, result)


def from_following(x, by):
    windows, tiles = lax.axis_size("win"), lax.axis_size("tile")
    pairs = [(w * tiles + t, (w - 1) * tiles + (t + by) % tiles) for w in range(1, windows) for t in range(tiles)]
    return lax.ppermute(x, ("win", "tile"), pairs)


def body(state, obs_weight, trajectory, coupling, prec_scale):
    own_state = state[0, 0]
    levels = own_state.shape[1] // GROUP
    cell = own_state.shape[2:]
    winds = trajectory[0, 0].reshape((2 * STEPS,) + own_state.shape[1:]).astype(jnp.float32)
    fields = VARS * levels
    window_index = lax.axis_index("win")
    last_window = lax.axis_size("win") - 1
    window = jnp.stack([window_index, jnp.int32(last_window)]).astype(jnp.int32)
    prec = lax.dynamic_slice_in_dim(prec_scale, (lax.axis_index("tile") % GROUP) * levels, levels, axis=1)

    def by_level(x):
        kinds = x.shape[0]
        x = x.reshape((kinds, GROUP, levels) + cell)
        return jnp.moveaxis(x, 1, 0).reshape((GROUP, kinds * levels) + cell)

    slab = exchange(by_level(jnp.concatenate([own_state, winds])))
    smem = pl.BlockSpec(memory_space=pltpu.SMEM)
    vmem = pl.BlockSpec(memory_space=pltpu.VMEM)
    core_shape = jax.ShapeDtypeStruct((GROUP, fields) + cell, jnp.float32)
    halo_shape = jax.ShapeDtypeStruct((HALO, fields) + cell, jnp.float32)
    slab_shapes = (halo_shape, core_shape, halo_shape)
    slab_scratch = [pltpu.VMEM(x.shape, x.dtype) for x in slab_shapes]
    params = pltpu.CompilerParams(vmem_limit_bytes=12 * 2**20)

    def cost(flops, moved_bytes):
        return pl.CostEstimate(flops=flops, bytes_accessed=moved_bytes, transcendentals=0)

    def flat(n):
        return jax.ShapeDtypeStruct((n,) + cell, jnp.float32)

    count = slab.shape[1]
    packed = flat(TY * count + pl.cdiv(count, SLOTS))
    follow_packed = flat((TY + 1) * (fields // 2) + pl.cdiv(fields, SLOTS))
    east_going, west_going, follow_east_going, follow_west_going = pl.pallas_call(
        functools.partial(pack_kernel, fields),
        out_shape=(packed, packed, follow_packed, follow_packed),
        in_specs=[vmem],
        out_specs=(vmem,) * 4,
        compiler_params=params,
        name="pack",
    )(slab)
    parts = (shifted(east_going, "tile", GROUP), slab, shifted(west_going, "tile", -GROUP))
    follow_parts = (
        from_following(follow_east_going, GROUP),
        passed_along(slab[:, :fields], "win", -1),
        from_following(follow_west_going, -GROUP),
    )
    corner = pltpu.VMEM((count,) + cell, jnp.float32)
    *moved, weighed = pl.pallas_call(
        functools.partial(forward_kernel, levels),
        out_shape=slab_shapes + (core_shape,),
        in_specs=[smem] * 3 + [vmem] * 3 + [pl.BlockSpec(memory_space=pl.ANY)] * 2,
        out_specs=(vmem,) * 4,
        scratch_shapes=slab_scratch * 2 + [corner] * 2,
        compiler_params=params,
        cost_estimate=cost(10_000_000, 12_000_000),
        name="forward",
    )(window, coupling, prec, *parts, follow_parts[0], follow_parts[2])
    earlier = passed_along(weighed, "win", 1)
    partial = pl.pallas_call(
        functools.partial(backward_kernel, levels),
        out_shape=core_shape,
        in_specs=[smem] * 3 + [vmem] * 9,
        out_specs=vmem,
        scratch_shapes=slab_scratch * 2 + [corner] * 2,
        compiler_params=params,
        cost_estimate=cost(12_000_000, 14_000_000),
        name="backward",
    )(window, coupling, prec, *follow_parts, *moved, *parts)
    back = exchange(partial - earlier)
    back = jnp.moveaxis(back.reshape((GROUP, VARS, levels) + cell), 0, 1).reshape(own_state.shape)
    return (back + obs_weight[0, 0] * own_state)[None, None]


def solution(mesh):
    in_specs = (
        P("win", "tile", None, None, None, None),
        P("win", "tile", None, None, None, None),
        P("win", "tile", None, None, None, None, None),
        P(),
        P(),
    )
    out_specs = P("win", "tile", None, None, None, None)
    return jax.shard_map(body, mesh=mesh, in_specs=in_specs, out_specs=out_specs, check_vma=False)
```

```python
import functools

import jax
import jax.numpy as jnp
from jax import lax
from jax.experimental import pallas as pl
from jax.experimental.pallas import tpu as pltpu
from jax.sharding import PartitionSpec as P

VARS = 5
STEPS = 3
GROUP = 16
TY = 4
HALO = TY + 1
CORNER = 8
smooth_weight = 0.2


def passed_along(x, axis, by):
    devices = lax.axis_size(axis)
    pairs = [(i, i + by) for i in range(devices) if 0 <= i + by < devices]
    return lax.ppermute(x, axis, pairs)


def shifted(x, axis, by):
    devices = lax.axis_size(axis)
    return lax.ppermute(x, axis, [(i, (i + by) % devices) for i in range(devices)])


def exchange(x):
    groups = [[first + i for i in range(GROUP)] for first in range(0, lax.axis_size("tile"), GROUP)]
    return lax.all_to_all(x, "tile", 0, 0, axis_index_groups=groups, tiled=True)


def masks():
    row = lax.broadcasted_iota(jnp.int32, (8, 128), 0)
    lane = lax.broadcasted_iota(jnp.int32, (8, 128), 1)
    return row == 0, row == 7, lane == 0, lane == 127


def east(sel, here, there):
    return pltpu.roll(jnp.where(sel[0], there, here), 7, 0)


def west(sel, here, there):
    return pltpu.roll(jnp.where(sel[1], there, here), 1, 0)


def north(sel, here, there):
    return pltpu.roll(jnp.where(sel[2], there, here), 127, 1)


def south(sel, here, there):
    return pltpu.roll(jnp.where(sel[3], there, here), 1, 1)


def mixed(coupling, values, a, transposed):
    terms = [(coupling[b, a] if transposed else coupling[a, b]) * values[b] for b in range(VARS)]
    return ((terms[0] + terms[1]) + (terms[2] + terms[3])) + terms[4]


class Slab:
    def __init__(self, parts, first=0):
        self.parts, self.first = parts, first

    def __getitem__(self, at):
        j, k = at
        ref, n = self.place(j)
        return ref[n, self.first + k]

    def place(self, j):
        west_part, own, east_part = self.parts
        if j < 0:
            return west_part, max(j + HALO, 0)
        if j < GROUP:
            return own, j
        return east_part, min(j - GROUP, HALO - 1)

    def put(self, j, k, value):
        ref, n = self.place(j)
        ref[n, k] = value


class Received:
    def __init__(self, west_packed, west_corner, own, east_packed, east_corner, first=0):
        self.west, self.east = (west_packed, west_corner), (east_packed, east_corner)
        self.own, self.first, self.planes = own, first, own.shape[1]

    def __getitem__(self, at):
        j, k = at[0], self.first + at[1]
        if j < -TY:
            return self.west[1][k]
        if j < 0:
            return self.west[0][(j + TY) * self.planes + k]
        if j < GROUP:
            return self.own[j, k]
        if j < GROUP + TY:
            return self.east[0][(j - GROUP) * self.planes + k]
        return self.east[1][k]


def tangent_step(levels, sel, coupling, src, winds, step, tiles, emit):
    @pl.loop(0, levels)
    def _(lv):
        for j in tiles:
            u = winds[j, 2 * step * levels + lv]
            v = winds[j, (2 * step + 1) * levels + lv]
            f = [src[j, a * levels + lv] for a in range(VARS)]
            for a in range(VARS):
                k = a * levels + lv
                dx = east(sel, f[a], src[j + TY, k]) - west(sel, f[a], src[j - TY, k])
                dy = north(sel, f[a], src[j + 1, k]) - south(sel, f[a], src[j - 1, k])
                emit(j, k, (f[a] + mixed(coupling, f, a, False)) + (u * dx + v * dy))


def adjoint_step(levels, sel, coupling, src, winds, step, tiles, emit):
    @pl.loop(0, levels)
    def _(lv):
        ku = 2 * step * levels + lv
        kv = (2 * step + 1) * levels + lv
        for j in tiles:
            ue = east(sel, winds[j, ku], winds[j + TY, ku])
            uw = west(sel, winds[j, ku], winds[j - TY, ku])
            vn = north(sel, winds[j, kv], winds[j + 1, kv])
            vs = south(sel, winds[j, kv], winds[j - 1, kv])
            g = [src[j, a * levels + lv] for a in range(VARS)]
            for a in range(VARS):
                k = a * levels + lv
                flux = uw * west(sel, g[a], src[j - TY, k]) - ue * east(sel, g[a], src[j + TY, k])
                flux += vs * south(sel, g[a], src[j - 1, k]) - vn * north(sel, g[a], src[j + 1, k])
                emit(j, k, (g[a] + mixed(coupling, g, a, True)) + flux)


def precision_step(levels, sel, prec, src, tiles, emit):
    @pl.loop(0, levels)
    def _(lv):
        for j in tiles:
            for a in range(VARS):
                k = a * levels + lv
                f = src[j, k]
                around = east(sel, f, src[j + TY, k]) + west(sel, f, src[j - TY, k])
                around += north(sel, f, src[j + 1, k]) + south(sel, f, src[j - 1, k])
                emit(j, k, prec[a, lv] * ((1.0 + 4.0 * smooth_weight) * f - smooth_weight * around))


OWN = range(GROUP)
WEST, EAST = range(-HALO, 0), range(GROUP, GROUP + HALO)
ALL = range(-HALO, GROUP + HALO)


def put_in(ref):
    def emit(j, k, value):
        ref[j, k] = value

    return emit


SLOTS = 128 // CORNER


def pack_corner(tile, out, at, shift):
    slot = lax.broadcasted_iota(jnp.int32, (8, 128), 1) // CORNER
    for first in range(0, len(tile), SLOTS):
        packed = jnp.zeros((8, 128), jnp.float32)
        for q, plane in enumerate(tile[first : first + SLOTS]):
            packed = jnp.where(slot == q, pltpu.roll(plane, (CORNER * q + shift) % 128, 1), packed)
        out[at + first // SLOTS] = packed


def unpack_corner(packed, at, out, shift):
    for k in range(out.shape[0]):
        out[k] = pltpu.roll(packed[at + k // SLOTS], (-CORNER * (k % SLOTS) - shift) % 128, 1)


def pack_kernel(fields, own, east_going, west_going, follow_east_going, follow_west_going):
    top = lax.broadcasted_iota(jnp.int32, (8, 128), 0) < 4
    count = own.shape[1]
    half = fields // 2
    for out, follow_out, first, paired, whole, corner, shift in (
        (east_going, follow_east_going, GROUP - TY, GROUP - TY, GROUP - 1, GROUP - HALO, CORNER),
        (west_going, follow_west_going, 0, 1, 0, TY, 0),
    ):
        for n in range(TY):
            out[pl.ds(n * count, count)] = own[first + n]
        follow_out[pl.ds((TY - 1) * half, fields)] = own[whole, pl.ds(0, fields)]
        for n in range(TY - 1):
            for k in range(0, fields, 2):
                one, two = own[paired + n, k], own[paired + n, k + 1]
                if shift:
                    pair = jnp.where(top, pltpu.roll(one, 4, 0), two)
                else:
                    pair = jnp.where(top, one, pltpu.roll(two, 4, 0))
                follow_out[n * half + k // 2] = pair
        tile = [own[corner, k] for k in range(count)]
        pack_corner(tile, out, TY * count, shift)
        pack_corner(tile[:fields], follow_out, (TY + 1) * half, shift)


def put_in(ref):
    def emit(j, k, value):
        ref[j, k] = value

    return emit


def received(west_in, own_in, east_in, west_corner, east_corner, first):
    at = TY * own_in.shape[1]
    unpack_corner(west_in, at, west_corner, CORNER)
    unpack_corner(east_in, at, east_corner, 0)
    return [Received(west_in, west_corner, own_in, east_in, east_corner, f) for f in (0, first)]


def forward_kernel(levels, window, coupling, prec, west_in, own_in, east_in, *refs):
    sel = masks()
    moved, own_weighted, f0, f1 = Slab(refs[:3]), refs[3], Slab(refs[4:7]), Slab(refs[7:10])
    state, winds = received(west_in, own_in, east_in, *refs[10:12], VARS * levels)

    @pl.when(window[0] != window[1])
    def _():
        tangent_step(levels, sel, coupling, state, winds, 0, ALL, f0.put)
        tangent_step(levels, sel, coupling, f0, winds, 1, ALL, f1.put)
        tangent_step(levels, sel, coupling, f1, winds, 2, ALL, moved.put)

    precision_step(levels, sel, prec, state, OWN, put_in(own_weighted))


def weigh_kernel(levels, window, prec, west_in, own_in, east_in, first, second, weighed):
    @pl.when(window[0] != window[1])
    def _():
        precision_step(levels, masks(), prec, Slab((west_in, own_in, east_in)), OWN, put_in(weighed))


def backward_kernel(levels, window, coupling, prec, follow_west, follow_own, follow_east, *refs):
    sel = masks()
    moved, own_weighted, out = Slab(refs[:3]), refs[3], refs[7]
    f0, f1 = Slab(refs[8:11]), Slab(refs[11:14])
    _, winds = received(*refs[4:7], *refs[14:16], VARS * levels)
    fields = VARS * levels

    @pl.when(window[0] == window[1])
    def _():
        out[...] = own_weighted[...]

    @pl.when(window[0] != window[1])
    def _():
        def result(j, k, value):
            out[j, k] = own_weighted[j, k] - value

        half = fields // 2
        for k in range(fields):
            for n in range(TY - 1):
                west_pair, east_pair = follow_west[n * half + k // 2], follow_east[n * half + k // 2]
                if k % 2 == 0:
                    west_pair = pltpu.roll(west_pair, 4, 0)
                else:
                    east_pair = pltpu.roll(east_pair, 4, 0)
                f1.put(n - TY, k, west_pair - moved[n - TY, k])
                f1.put(GROUP + 1 + n, k, east_pair - moved[GROUP + 1 + n, k])
            f1.put(-1, k, follow_west[(TY - 1) * half + k] - moved[-1, k])
            f1.put(GROUP, k, follow_east[(TY - 1) * half + k] - moved[GROUP, k])
            at, turn = (TY + 1) * half + k // SLOTS, CORNER * (k % SLOTS)
            f1.put(-HALO, k, pltpu.roll(follow_west[at], (-turn - CORNER) % 128, 1) - moved[-HALO, k])
            f1.put(GROUP + TY, k, pltpu.roll(follow_east[at], -turn % 128, 1) - moved[GROUP + TY, k])

        @pl.loop(0, fields)
        def _(k):
            for j in OWN:
                f1.put(j, k, follow_own[j, k] - moved[j, k])

        precision_step(levels, sel, prec, f1, ALL, f0.put)
        adjoint_step(levels, sel, coupling, f0, winds, 2, ALL, f1.put)
        adjoint_step(levels, sel, coupling, f1, winds, 1, ALL[1:-1], f0.put)
        adjoint_step(levels, sel, coupling, f0, winds, 0, OWN, result)


def from_following(x, by):
    windows, tiles = lax.axis_size("win"), lax.axis_size("tile")
    pairs = [(w * tiles + t, (w - 1) * tiles + (t + by) % tiles) for w in range(1, windows) for t in range(tiles)]
    return lax.ppermute(x, ("win", "tile"), pairs)


def body(state, obs_weight, trajectory, coupling, prec_scale):
    own_state = state[0, 0]
    levels = own_state.shape[1] // GROUP
    cell = own_state.shape[2:]
    winds = trajectory[0, 0].reshape((2 * STEPS,) + own_state.shape[1:]).astype(jnp.float32)
    fields = VARS * levels
    window_index = lax.axis_index("win")
    last_window = lax.axis_size("win") - 1
    window = jnp.stack([window_index, jnp.int32(last_window)]).astype(jnp.int32)
    prec = lax.dynamic_slice_in_dim(prec_scale, (lax.axis_index("tile") % GROUP) * levels, levels, axis=1)

    def by_level(x):
        kinds = x.shape[0]
        x = x.reshape((kinds, GROUP, levels) + cell)
        return jnp.moveaxis(x, 1, 0).reshape((GROUP, kinds * levels) + cell)

    slab = exchange(by_level(jnp.concatenate([own_state, winds])))
    smem = pl.BlockSpec(memory_space=pltpu.SMEM)
    vmem = pl.BlockSpec(memory_space=pltpu.VMEM)
    core_shape = jax.ShapeDtypeStruct((GROUP, fields) + cell, jnp.float32)
    halo_shape = jax.ShapeDtypeStruct((HALO, fields) + cell, jnp.float32)
    slab_shapes = (halo_shape, core_shape, halo_shape)
    slab_scratch = [pltpu.VMEM(x.shape, x.dtype) for x in slab_shapes]
    params = pltpu.CompilerParams(vmem_limit_bytes=12 * 2**20)

    def cost(flops, moved_bytes):
        return pl.CostEstimate(flops=flops, bytes_accessed=moved_bytes, transcendentals=0)

    def flat(n):
        return jax.ShapeDtypeStruct((n,) + cell, jnp.float32)

    count = slab.shape[1]
    packed = flat(TY * count + pl.cdiv(count, SLOTS))
    follow_packed = flat((TY + 1) * (fields // 2) + pl.cdiv(fields, SLOTS))
    east_going, west_going, follow_east_going, follow_west_going = pl.pallas_call(
        functools.partial(pack_kernel, fields),
        out_shape=(packed, packed, follow_packed, follow_packed),
        in_specs=[vmem],
        out_specs=(vmem,) * 4,
        compiler_params=params,
        name="pack",
    )(slab)
    parts = (shifted(east_going, "tile", GROUP), slab, shifted(west_going, "tile", -GROUP))
    follow_parts = (
        from_following(follow_east_going, GROUP),
        passed_along(slab[:, :fields], "win", -1),
        from_following(follow_west_going, -GROUP),
    )
    corner = pltpu.VMEM((count,) + cell, jnp.float32)
    *moved, own_weighted = pl.pallas_call(
        functools.partial(forward_kernel, levels),
        out_shape=slab_shapes + (core_shape,),
        in_specs=[smem] * 3 + [vmem] * 3,
        out_specs=(vmem,) * 4,
        scratch_shapes=slab_scratch * 2 + [corner] * 2,
        compiler_params=params,
        cost_estimate=cost(10_000_000, 12_000_000),
        name="forward",
    )(window, coupling, prec, *parts)
    weighed = pl.pallas_call(
        functools.partial(weigh_kernel, levels),
        out_shape=core_shape,
        in_specs=[smem] * 2 + [vmem] * 3 + [pl.BlockSpec(memory_space=pl.ANY)] * 2,
        out_specs=vmem,
        compiler_params=params,
        cost_estimate=cost(2_000_000, 2_000_000),
        name="weigh",
    )(window, prec, *moved, follow_parts[0], follow_parts[2])
    earlier = passed_along(weighed, "win", 1)
    partial = pl.pallas_call(
        functools.partial(backward_kernel, levels),
        out_shape=core_shape,
        in_specs=[smem] * 3 + [vmem] * 10,
        out_specs=vmem,
        scratch_shapes=slab_scratch * 2 + [corner] * 2,
        compiler_params=params,
        cost_estimate=cost(12_000_000, 14_000_000),
        name="backward",
    )(window, coupling, prec, *follow_parts, *moved, own_weighted, *parts)
    back = exchange(partial - earlier)
    back = jnp.moveaxis(back.reshape((GROUP, VARS, levels) + cell), 0, 1).reshape(own_state.shape)
    return (back + obs_weight[0, 0] * own_state)[None, None]


def solution(mesh):
    in_specs = (
        P("win", "tile", None, None, None, None),
        P("win", "tile", None, None, None, None),
        P("win", "tile", None, None, None, None, None),
        P(),
        P(),
    )
    out_specs = P("win", "tile", None, None, None, None)
    return jax.shard_map(body, mesh=mesh, in_specs=in_specs, out_specs=out_specs, check_vma=False)
```

```python
import functools

import jax
import jax.numpy as jnp
from jax import lax
from jax.experimental import pallas as pl
from jax.experimental.pallas import tpu as pltpu
from jax.sharding import PartitionSpec as P

VARS = 5
STEPS = 3
GROUP = 16
TY = 4
HALO = TY + 1
CORNER = 8
smooth_weight = 0.2


def passed_along(x, axis, by):
    devices = lax.axis_size(axis)
    pairs = [(i, i + by) for i in range(devices) if 0 <= i + by < devices]
    return lax.ppermute(x, axis, pairs)


def shifted(x, axis, by):
    devices = lax.axis_size(axis)
    return lax.ppermute(x, axis, [(i, (i + by) % devices) for i in range(devices)])


def exchange(x):
    groups = [[first + i for i in range(GROUP)] for first in range(0, lax.axis_size("tile"), GROUP)]
    return lax.all_to_all(x, "tile", 0, 0, axis_index_groups=groups, tiled=True)


def masks():
    row = lax.broadcasted_iota(jnp.int32, (8, 128), 0)
    lane = lax.broadcasted_iota(jnp.int32, (8, 128), 1)
    return row == 0, row == 7, lane == 0, lane == 127


def east(sel, here, there):
    return pltpu.roll(jnp.where(sel[0], there, here), 7, 0)


def west(sel, here, there):
    return pltpu.roll(jnp.where(sel[1], there, here), 1, 0)


def north(sel, here, there):
    return pltpu.roll(jnp.where(sel[2], there, here), 127, 1)


def south(sel, here, there):
    return pltpu.roll(jnp.where(sel[3], there, here), 1, 1)


def mixed(coupling, values, a, transposed):
    terms = [(coupling[b, a] if transposed else coupling[a, b]) * values[b] for b in range(VARS)]
    return ((terms[0] + terms[1]) + (terms[2] + terms[3])) + terms[4]


class Slab:
    def __init__(self, parts, first=0):
        self.parts, self.first = parts, first

    def __getitem__(self, at):
        j, k = at
        ref, n = self.place(j)
        return ref[n, self.first + k]

    def place(self, j):
        west_part, own, east_part = self.parts
        if j < 0:
            return west_part, max(j + HALO, 0)
        if j < GROUP:
            return own, j
        return east_part, min(j - GROUP, HALO - 1)

    def put(self, j, k, value):
        ref, n = self.place(j)
        ref[n, k] = value


class Received:
    def __init__(self, west, own, east, first, keep):
        self.west, self.own, self.east, self.first, self.keep = west, own, east, first, keep

    def halo(self, side, n, whole, k):
        packed, corner, tail = side
        if whole:
            return packed[(TY - 1) * self.keep + k]
        return packed[n * self.keep + k] if k < self.keep else tail[n, k - self.keep]

    def __getitem__(self, at):
        j, k = at[0], self.first + at[1]
        if j < -TY:
            return self.west[1][k]
        if j < 0:
            return self.halo(self.west, j + TY, j == -1, k)
        if j < GROUP:
            return self.own[j, k]
        if j < GROUP + TY:
            return self.halo(self.east, j - GROUP - 1, j == GROUP, k)
        return self.east[1][k]


def tangent_step(levels, sel, coupling, src, winds, step, tiles, emit):
    for lv in range(levels):
        for j in tiles:
            u = winds[j, 2 * step * levels + lv]
            v = winds[j, (2 * step + 1) * levels + lv]
            f = [src[j, a * levels + lv] for a in range(VARS)]
            for a in range(VARS):
                k = a * levels + lv
                dx = east(sel, f[a], src[j + TY, k]) - west(sel, f[a], src[j - TY, k])
                dy = north(sel, f[a], src[j + 1, k]) - south(sel, f[a], src[j - 1, k])
                emit(j, k, (f[a] + mixed(coupling, f, a, False)) + (u * dx + v * dy))


def adjoint_step(levels, sel, coupling, src, winds, step, tiles, emit):
    for lv in range(levels):
        ku = 2 * step * levels + lv
        kv = (2 * step + 1) * levels + lv
        for j in tiles:
            ue = east(sel, winds[j, ku], winds[j + TY, ku])
            uw = west(sel, winds[j, ku], winds[j - TY, ku])
            vn = north(sel, winds[j, kv], winds[j + 1, kv])
            vs = south(sel, winds[j, kv], winds[j - 1, kv])
            g = [src[j, a * levels + lv] for a in range(VARS)]
            for a in range(VARS):
                k = a * levels + lv
                flux = uw * west(sel, g[a], src[j - TY, k]) - ue * east(sel, g[a], src[j + TY, k])
                flux += vs * south(sel, g[a], src[j - 1, k]) - vn * north(sel, g[a], src[j + 1, k])
                emit(j, k, (g[a] + mixed(coupling, g, a, True)) + flux)


def precision_step(levels, sel, prec, src, tiles, emit):
    for lv in range(levels):
        for j in tiles:
            for a in range(VARS):
                k = a * levels + lv
                f = src[j, k]
                around = east(sel, f, src[j + TY, k]) + west(sel, f, src[j - TY, k])
                around += north(sel, f, src[j + 1, k]) + south(sel, f, src[j - 1, k])
                emit(j, k, prec[a, lv] * ((1.0 + 4.0 * smooth_weight) * f - smooth_weight * around))


OWN = range(GROUP)
WEST, EAST = range(-HALO, 0), range(GROUP, GROUP + HALO)
ALL = range(-HALO, GROUP + HALO)


def put_in(ref):
    def emit(j, k, value):
        ref[j, k] = value

    return emit


SLOTS = 128 // CORNER


def pack_corner(tile, out, at, shift):
    slot = lax.broadcasted_iota(jnp.int32, (8, 128), 1) // CORNER
    for first in range(0, len(tile), SLOTS):
        packed = jnp.zeros((8, 128), jnp.float32)
        for q, plane in enumerate(tile[first : first + SLOTS]):
            packed = jnp.where(slot == q, pltpu.roll(plane, (CORNER * q + shift) % 128, 1), packed)
        out[at + first // SLOTS] = packed


def unpack_corner(packed, at, out, shift):
    for k in range(out.shape[0]):
        out[k] = pltpu.roll(packed[at + k // SLOTS], (-CORNER * (k % SLOTS) - shift) % 128, 1)


def kept(fields):
    tail = 2 * fields // VARS
    return fields + (STEPS - 1) * tail, tail


def pack_kernel(fields, own, east_going, west_going, follow_east_going, follow_west_going):
    row = lax.broadcasted_iota(jnp.int32, (8, 128), 0)
    top = row < 4
    count = own.shape[1]
    keep, tail = kept(fields)
    half = fields // 2
    for out, follow_out, paired, whole, corner, shift in (
        (east_going, follow_east_going, GROUP - TY, GROUP - 1, GROUP - HALO, CORNER),
        (west_going, follow_west_going, 1, 0, TY, 0),
    ):
        for n in range(TY - 1):
            out[pl.ds(n * keep, keep)] = own[paired + n, pl.ds(0, keep)]
            for k in range(tail):
                last = own[paired + n, keep + k]
                for step, turn in enumerate((2, 4) if shift else (6, 4)):
                    at = fields + step * tail + k
                    free = row < 2 if shift else row >= 6
                    out[n * keep + at] = jnp.where(free, pltpu.roll(last, turn, 0), own[paired + n, at])
        out[pl.ds((TY - 1) * keep, count)] = own[whole]
        follow_out[pl.ds((TY - 1) * half, fields)] = own[whole, pl.ds(0, fields)]
        for n in range(TY - 1):
            for k in range(0, fields, 2):
                one, two = own[paired + n, k], own[paired + n, k + 1]
                if shift:
                    pair = jnp.where(top, pltpu.roll(one, 4, 0), two)
                else:
                    pair = jnp.where(top, one, pltpu.roll(two, 4, 0))
                follow_out[n * half + k // 2] = pair
        tile = [own[corner, k] for k in range(count)]
        pack_corner(tile, out, (TY - 1) * keep + count, shift)
        pack_corner(tile[:fields], follow_out, (TY + 1) * half, shift)


def put_in(ref):
    def emit(j, k, value):
        ref[j, k] = value

    return emit


def received(west_in, own_in, east_in, scratch, fields):
    row = lax.broadcasted_iota(jnp.int32, (8, 128), 0)
    keep, tail = kept(fields)
    west_corner, east_corner, west_tail, east_tail = scratch
    at = (TY - 1) * keep + own_in.shape[1]
    unpack_corner(west_in, at, west_corner, CORNER)
    unpack_corner(east_in, at, east_corner, 0)
    for n in range(TY - 1):
        for k in range(tail):
            one, two = n * keep + fields + k, n * keep + fields + tail + k
            west_tail[n, k] = jnp.where(row >= 6, pltpu.roll(west_in[one], 6, 0), pltpu.roll(west_in[two], 4, 0))
            east_tail[n, k] = jnp.where(row < 2, pltpu.roll(east_in[one], 2, 0), pltpu.roll(east_in[two], 4, 0))
    west, east = (west_in, west_corner, west_tail), (east_in, east_corner, east_tail)
    return [Received(west, own_in, east, first, keep) for first in (0, fields)]


def forward_kernel(levels, window, coupling, prec, west_in, own_in, east_in, *refs):
    sel = masks()
    moved, own_weighted, f0, f1 = Slab(refs[:3]), refs[3], Slab(refs[4:7]), Slab(refs[7:10])
    state, winds = received(west_in, own_in, east_in, refs[10:14], VARS * levels)

    @pl.when(window[0] != window[1])
    def _():
        tangent_step(levels, sel, coupling, state, winds, 0, ALL, f0.put)
        tangent_step(levels, sel, coupling, f0, winds, 1, ALL, f1.put)
        tangent_step(levels, sel, coupling, f1, winds, 2, ALL, moved.put)

    precision_step(levels, sel, prec, state, OWN, put_in(own_weighted))


def weigh_kernel(levels, window, prec, west_in, own_in, east_in, first, second, weighed):
    @pl.when(window[0] != window[1])
    def _():
        precision_step(levels, masks(), prec, Slab((west_in, own_in, east_in)), OWN, put_in(weighed))


def backward_kernel(levels, window, coupling, prec, follow_west, follow_own, follow_east, *refs):
    sel = masks()
    moved, own_weighted, out = Slab(refs[:3]), refs[3], refs[7]
    f0, f1 = Slab(refs[8:11]), Slab(refs[11:14])
    _, winds = received(*refs[4:7], refs[14:18], VARS * levels)
    fields = VARS * levels

    @pl.when(window[0] == window[1])
    def _():
        out[...] = own_weighted[...]

    @pl.when(window[0] != window[1])
    def _():
        def result(j, k, value):
            out[j, k] = own_weighted[j, k] - value

        half = fields // 2
        for k in range(fields):
            for n in range(TY - 1):
                west_pair, east_pair = follow_west[n * half + k // 2], follow_east[n * half + k // 2]
                if k % 2 == 0:
                    west_pair = pltpu.roll(west_pair, 4, 0)
                else:
                    east_pair = pltpu.roll(east_pair, 4, 0)
                f1.put(n - TY, k, west_pair - moved[n - TY, k])
                f1.put(GROUP + 1 + n, k, east_pair - moved[GROUP + 1 + n, k])
            f1.put(-1, k, follow_west[(TY - 1) * half + k] - moved[-1, k])
            f1.put(GROUP, k, follow_east[(TY - 1) * half + k] - moved[GROUP, k])
            at, turn = (TY + 1) * half + k // SLOTS, CORNER * (k % SLOTS)
            f1.put(-HALO, k, pltpu.roll(follow_west[at], (-turn - CORNER) % 128, 1) - moved[-HALO, k])
            f1.put(GROUP + TY, k, pltpu.roll(follow_east[at], -turn % 128, 1) - moved[GROUP + TY, k])

        @pl.loop(0, fields)
        def _(k):
            for j in OWN:
                f1.put(j, k, follow_own[j, k] - moved[j, k])

        precision_step(levels, sel, prec, f1, ALL, f0.put)
        adjoint_step(levels, sel, coupling, f0, winds, 2, ALL, f1.put)
        adjoint_step(levels, sel, coupling, f1, winds, 1, ALL[1:-1], f0.put)
        adjoint_step(levels, sel, coupling, f0, winds, 0, OWN, result)


def from_following(x, by):
    windows, tiles = lax.axis_size("win"), lax.axis_size("tile")
    pairs = [(w * tiles + t, (w - 1) * tiles + (t + by) % tiles) for w in range(1, windows) for t in range(tiles)]
    return lax.ppermute(x, ("win", "tile"), pairs)


def body(state, obs_weight, trajectory, coupling, prec_scale):
    own_state = state[0, 0]
    levels = own_state.shape[1] // GROUP
    cell = own_state.shape[2:]
    winds = trajectory[0, 0].reshape((2 * STEPS,) + own_state.shape[1:]).astype(jnp.float32)
    fields = VARS * levels
    window_index = lax.axis_index("win")
    last_window = lax.axis_size("win") - 1
    window = jnp.stack([window_index, jnp.int32(last_window)]).astype(jnp.int32)
    prec = lax.dynamic_slice_in_dim(prec_scale, (lax.axis_index("tile") % GROUP) * levels, levels, axis=1)

    def by_level(x):
        kinds = x.shape[0]
        x = x.reshape((kinds, GROUP, levels) + cell)
        return jnp.moveaxis(x, 1, 0).reshape((GROUP, kinds * levels) + cell)

    slab = exchange(by_level(jnp.concatenate([own_state, winds])))
    smem = pl.BlockSpec(memory_space=pltpu.SMEM)
    vmem = pl.BlockSpec(memory_space=pltpu.VMEM)
    core_shape = jax.ShapeDtypeStruct((GROUP, fields) + cell, jnp.float32)
    halo_shape = jax.ShapeDtypeStruct((HALO, fields) + cell, jnp.float32)
    slab_shapes = (halo_shape, core_shape, halo_shape)
    slab_scratch = [pltpu.VMEM(x.shape, x.dtype) for x in slab_shapes]
    params = pltpu.CompilerParams(vmem_limit_bytes=12 * 2**20)

    def cost(flops, moved_bytes):
        return pl.CostEstimate(flops=flops, bytes_accessed=moved_bytes, transcendentals=0)

    def flat(n):
        return jax.ShapeDtypeStruct((n,) + cell, jnp.float32)

    count = slab.shape[1]
    keep, tail = kept(fields)
    packed = flat((TY - 1) * keep + count + pl.cdiv(count, SLOTS))
    follow_packed = flat((TY + 1) * (fields // 2) + pl.cdiv(fields, SLOTS))
    east_going, west_going, follow_east_going, follow_west_going = pl.pallas_call(
        functools.partial(pack_kernel, fields),
        out_shape=(packed, packed, follow_packed, follow_packed),
        in_specs=[vmem],
        out_specs=(vmem,) * 4,
        compiler_params=params,
        name="pack",
    )(slab)
    parts = (shifted(east_going, "tile", GROUP), slab, shifted(west_going, "tile", -GROUP))
    follow_parts = (
        from_following(follow_east_going, GROUP),
        passed_along(slab[:, :fields], "win", -1),
        from_following(follow_west_going, -GROUP),
    )
    unpacked = [pltpu.VMEM((count,) + cell, jnp.float32)] * 2 + [pltpu.VMEM((TY - 1, tail) + cell, jnp.float32)] * 2
    *moved, own_weighted = pl.pallas_call(
        functools.partial(forward_kernel, levels),
        out_shape=slab_shapes + (core_shape,),
        in_specs=[smem] * 3 + [vmem] * 3,
        out_specs=(vmem,) * 4,
        scratch_shapes=slab_scratch * 2 + unpacked,
        compiler_params=params,
        cost_estimate=cost(10_000_000, 12_000_000),
        name="forward",
    )(window, coupling, prec, *parts)
    weighed = pl.pallas_call(
        functools.partial(weigh_kernel, levels),
        out_shape=core_shape,
        in_specs=[smem] * 2 + [vmem] * 3 + [pl.BlockSpec(memory_space=pl.ANY)] * 2,
        out_specs=vmem,
        compiler_params=params,
        cost_estimate=cost(2_000_000, 2_000_000),
        name="weigh",
    )(window, prec, *moved, follow_parts[0], follow_parts[2])
    earlier = passed_along(weighed, "win", 1)
    partial = pl.pallas_call(
        functools.partial(backward_kernel, levels),
        out_shape=core_shape,
        in_specs=[smem] * 3 + [vmem] * 10,
        out_specs=vmem,
        scratch_shapes=slab_scratch * 2 + unpacked,
        compiler_params=params,
        cost_estimate=cost(12_000_000, 14_000_000),
        name="backward",
    )(window, coupling, prec, *follow_parts, *moved, own_weighted, *parts)
    back = exchange(partial - earlier)
    back = jnp.moveaxis(back.reshape((GROUP, VARS, levels) + cell), 0, 1).reshape(own_state.shape)
    return (back + obs_weight[0, 0] * own_state)[None, None]


def solution(mesh):
    in_specs = (
        P("win", "tile", None, None, None, None),
        P("win", "tile", None, None, None, None),
        P("win", "tile", None, None, None, None, None),
        P(),
        P(),
    )
    out_specs = P("win", "tile", None, None, None, None)
    return jax.shard_map(body, mesh=mesh, in_specs=in_specs, out_specs=out_specs, check_vma=False)
```
